32 devices in a mesh: ctx: 16 (over z, x, core), head: 2 (over y).
Axes of the slice: x: 2, y: 2, z: 4, core: 2. Of those that a mesh axis runs over, the one named last changes fastest.
Arguments:
- queries: float32 [16384, 2048], P('ctx', 'head'), may hold values from -5 to 5
- keys: float32 [16384, 2048], P('ctx', 'head'), may hold values from -5 to 5
- values: float32 [16384, 2048], P('ctx', 'head'), may hold values from -6 to 6
- stride_query_w: float32 [2048, 2048], P(None, 'head'), may hold values from -0.53033006 to 0.53033006
- stride_key_w: float32 [2048, 2048], P(None, 'head'), may hold values from -0.53033006 to 0.53033006
- stride_value_w: float32 [2048, 2048], P(None, 'head'), may hold values from -0.70710677 to 0.70710677
- out_weight: float32 [2048, 2048], P('head'), may hold values from -0.5 to 0.5
Outputs:
- mixed: float32 [16384, 2048], P(('ctx', 'head'))
The draws below stay inside these ranges and needn't reach their ends.
All inputs are finite; a program needn't handle non-finite values.
Results may differ from the reference program's by a relative error of at most 0.0003.
Values sent between devices are 32-bit elements; how exact they have to be, the bound alone decides.
A program may use at most 256 MiB of HBM per device.

```python
import jax
import jax.numpy as jnp
from jax import lax

HEADS = 16
HSZ = 128
BAND = 512
STRIDE = 512
SEQ = 16384
D = 2048


def draw_queries(key, part):
    base = jnp.clip(1.5 * jax.random.normal(jax.random.fold_in(key, 11), (SEQ, D), jnp.float32), -4.5, 4.5)
    return base


def draw_keys(key, part):
    base = jnp.clip(1.5 * jax.random.normal(jax.random.fold_in(key, 13), (SEQ, D), jnp.float32), -4.5, 4.5)
    return base


def block_scale(stream_key, shape, pieces, smallest, top_value):
    def one(axis_at, parts):
        steps = jax.random.uniform(jax.random.fold_in(jax.random.fold_in(stream_key, 6), axis_at), (parts,), jnp.float32, smallest / len(pieces), top_value / len(pieces))
        return jnp.repeat(jnp.exp(steps), shape[axis_at] // parts).reshape((-1,) + (1,) * (len(shape) - axis_at - 1))

    factor_of = one(*pieces[0])
    for cut in pieces[1:]:
        factor_of = factor_of * one(*cut)
    return factor_of


def scatter_about(own_key, dims, deviation, reach, split=(), held_as=jnp.bfloat16):
    array = deviation * jax.random.normal(own_key, dims, jnp.float32)
    if split:
        array = array * block_scale(own_key, dims, split, -0.22, 0.18)
    return jnp.clip(array, -reach, reach).astype(held_as)


def setup_inputs(seed: int = 0) -> dict:
    seeds = jax.random.split(jax.random.key(seed), 8)
    queries = draw_queries(jax.random.fold_in(seeds[7], 71), 0)
    keys = draw_keys(jax.random.fold_in(seeds[7], 71), 0)
    values = scatter_about(seeds[2], (SEQ, D), 1.0, 6.0, ((0, 16), (1, 2)), jnp.float32)
    stride_query_w = scatter_about(seeds[3], (D, D), (6.0 * D ** -0.5), 0.53033006, ((1, 2),), jnp.float32)
    stride_key_w = scatter_about(seeds[4], (D, D), (6.0 * D ** -0.5), 0.53033006, ((1, 2),), jnp.float32)
    stride_value_w = scatter_about(seeds[5], (D, D), (8.0 * D ** -0.5), 0.70710677, ((1, 2),), jnp.float32)
    out_weight = scatter_about(seeds[6], (D, D), HSZ ** -0.5, 0.5, ((0, 2),), jnp.float32)
    return {"queries": queries, "keys": keys, "values": values, "stride_query_w": stride_query_w, "stride_key_w": stride_key_w, "stride_value_w": stride_value_w, "out_weight": out_weight}


def band_block(q_rows, k_rows, v_rows, q_first, k_first):
    scores = jnp.einsum('qhd,khd->hqk', q_rows, k_rows, precision=lax.Precision.HIGHEST) * (HSZ ** -0.5)
    q_pos = q_first + jnp.arange(q_rows.shape[0], dtype=jnp.int32)[:, None]
    k_pos = k_first + jnp.arange(k_rows.shape[0], dtype=jnp.int32)[None, :]
    allowed = (k_pos <= q_pos) & (k_pos > q_pos - BAND) & (k_pos >= 0)
    scores = jnp.where(allowed[None], scores, -jnp.inf)
    top = jnp.max(scores, axis=-1, keepdims=True)
    weights = jnp.exp(scores - top)
    total = jnp.sum(weights, axis=-1)
    summed = jnp.einsum('hqk,khd->qhd', weights, v_rows, precision=lax.Precision.HIGHEST)
    return summed / jnp.transpose(total)[:, :, None]


def strided_one(q_two, k_two, v_two):
    scores = jnp.einsum('brd,crd->rbc', q_two, k_two, precision=lax.Precision.HIGHEST) * (HSZ ** -0.5)
    count = q_two.shape[0]
    allowed = jnp.arange(count, dtype=jnp.int32)[None, :] <= jnp.arange(count, dtype=jnp.int32)[:, None]
    scores = jnp.where(allowed[None], scores, -jnp.inf)
    top = jnp.max(scores, axis=-1, keepdims=True)
    weights = jnp.exp(scores - top)
    total = jnp.sum(weights, axis=-1)
    summed = jnp.einsum('rbc,crd->brd', weights, v_two, precision=lax.Precision.HIGHEST)
    return summed / jnp.transpose(total)[:, :, None]


def project(flat, matrix):
    product = jnp.dot(flat, matrix, precision=lax.Precision.HIGHEST, preferred_element_type=jnp.float32)
    return product.reshape(SEQ // STRIDE, STRIDE, HEADS, HSZ)


def reference(queries, keys, values, stride_query_w, stride_key_w, stride_value_w, out_weight):
    q_heads = queries.reshape(SEQ, HEADS, HSZ)
    pad = jnp.zeros((BAND, HEADS, HSZ), jnp.float32)
    key_ext = jnp.concatenate([pad, keys.reshape(SEQ, HEADS, HSZ)], axis=0)
    value_ext = jnp.concatenate([pad, values.reshape(SEQ, HEADS, HSZ)], axis=0)

    def one_block(index):
        offset = index * BAND
        q_rows = lax.dynamic_slice_in_dim(q_heads, offset, BAND, 0)
        k_rows = lax.dynamic_slice_in_dim(key_ext, offset, 2 * BAND, 0)
        v_rows = lax.dynamic_slice_in_dim(value_ext, offset, 2 * BAND, 0)
        return band_block(q_rows, k_rows, v_rows, offset, offset - BAND)

    banded = lax.map(one_block, jnp.arange(SEQ // BAND, dtype=jnp.int32)).reshape(SEQ, D)
    q_two = project(banded, stride_query_w)
    k_two = project(banded, stride_key_w)
    v_two = project(banded, stride_value_w)

    def per_head(trio):
        return strided_one(trio[0], trio[1], trio[2])

    heads_first = lax.map(per_head, (jnp.moveaxis(q_two, 2, 0), jnp.moveaxis(k_two, 2, 0), jnp.moveaxis(v_two, 2, 0)))
    strided = jnp.moveaxis(heads_first, 0, 2).reshape(SEQ, D)
    return jnp.dot(strided, out_weight, precision=lax.Precision.HIGHEST, preferred_element_type=jnp.float32)
```

```python
import jax
import jax.numpy as jnp
from jax import lax
from jax.sharding import PartitionSpec as P

HSZ = 128
BAND = 512
STRIDE = 512
HIGHEST = lax.Precision.HIGHEST


def passed_along(block, axis, distance):
    devices = range(lax.axis_size(axis))
    route = [(i - distance, i) for i in devices if i - distance in devices]
    return lax.ppermute(block, axis, route)


def band_block(q_rows, k_rows, v_rows, q_first, k_first):
    scores = jnp.einsum("qhd,khd->hqk", q_rows, k_rows, precision=HIGHEST) * HSZ ** (-0.5)
    q_pos = q_first + jnp.arange(q_rows.shape[0], dtype=jnp.int32)[:, None]
    k_pos = k_first + jnp.arange(k_rows.shape[0], dtype=jnp.int32)[None, :]
    allowed = (k_pos <= q_pos) & (k_pos > q_pos - BAND) & (k_pos >= 0)
    scores = jnp.where(allowed[None], scores, -jnp.inf)
    top = jnp.max(scores, axis=-1, keepdims=True)
    weights = jnp.exp(scores - top)
    total = jnp.sum(weights, axis=-1)
    summed = jnp.einsum("hqk,khd->qhd", weights, v_rows, precision=HIGHEST)
    return summed / jnp.transpose(total)[:, :, None]


def strided_one(q_two, k_two, v_two):
    scores = jnp.einsum("brd,crd->rbc", q_two, k_two, precision=HIGHEST) * HSZ ** (-0.5)
    count = q_two.shape[0]
    allowed = (
        jnp.arange(count, dtype=jnp.int32)[None, :] <= jnp.arange(count, dtype=jnp.int32)[:, None]
    )
    scores = jnp.where(allowed[None], scores, -jnp.inf)
    top = jnp.max(scores, axis=-1, keepdims=True)
    weights = jnp.exp(scores - top)
    total = jnp.sum(weights, axis=-1)
    summed = jnp.einsum("rbc,crd->brd", weights, v_two, precision=HIGHEST)
    return summed / jnp.transpose(total)[:, :, None]


def matmul(left, right):
    return jnp.dot(left, right, precision=HIGHEST, preferred_element_type=jnp.float32)


def local(queries, keys, values, stride_query_w, stride_key_w, stride_value_w, out_weight):
    rows, width = queries.shape
    heads_here = width // HSZ
    along, across = lax.axis_size("ctx"), lax.axis_size("head")
    own_rows = rows // across
    piece = own_rows // along
    first = lax.axis_index("ctx") * rows
    tails = jnp.stack([keys[rows - BAND :], values[rows - BAND :]])
    before = passed_along(tails, "ctx", 1)
    groups = 2 if heads_here % 2 == 0 else 1
    part = width // groups
    by_head = (-1, heads_here // groups, HSZ)
    maps = (stride_query_w, stride_key_w, stride_value_w)
    sums = [0.0, 0.0, 0.0]
    for group in range(groups):
        here = slice(group * part, (group + 1) * part)
        later = [
            band_block(
                queries[at : at + BAND, here].reshape(by_head),
                keys[at - BAND : at + BAND, here].reshape(by_head),
                values[at - BAND : at + BAND, here].reshape(by_head),
                first + at,
                first + at - BAND,
            )
            for at in range(BAND, rows, BAND)
        ]
        start = band_block(
            queries[:BAND, here].reshape(by_head),
            jnp.concatenate([before[0][:, here], keys[:BAND, here]], axis=0).reshape(by_head),
            jnp.concatenate([before[1][:, here], values[:BAND, here]], axis=0).reshape(by_head),
            first,
            first - BAND,
        )
        banded = jnp.concatenate([start] + later, axis=0).reshape(across, along, piece, part)
        banded = jnp.transpose(banded, (1, 0, 2, 3))
        banded = lax.all_to_all(banded, "ctx", split_axis=0, concat_axis=0, tiled=True)
        banded = lax.all_gather(banded.reshape(rows, part), "head", axis=1, tiled=True)
        for at, weight in enumerate(maps):
            met = weight.reshape(across, groups, part, width)[:, group].reshape(-1, width)
            sums[at] = sums[at] + matmul(banded, met)
    grouped = (along * (rows // STRIDE), STRIDE // along, heads_here, HSZ)
    q_two, k_two, v_two = (total.reshape(grouped) for total in sums)
    attended = jax.vmap(strided_one, in_axes=2, out_axes=2)(q_two, k_two, v_two)
    attended = attended.reshape(along, across, piece, width)
    attended = jnp.transpose(attended, (1, 0, 2, 3)).reshape(rows, width)
    columns = out_weight.shape[1] // 2
    halves = []
    for at in range(0, 2 * columns, columns):
        share = matmul(attended, out_weight[:, at : at + columns])
        mixed = lax.psum_scatter(share, "head", scatter_dimension=0, tiled=True)
        mixed = mixed.reshape(along, piece, columns)
        mixed = lax.all_to_all(mixed, "ctx", split_axis=0, concat_axis=0, tiled=True)
        halves.append(mixed.reshape(own_rows, columns))
    return jnp.concatenate(halves, axis=1)


def solution(mesh):
    return jax.shard_map(
        local,
        mesh=mesh,
        in_specs=(
            P("ctx", "head"),
            P("ctx", "head"),
            P("ctx", "head"),
            P(None, "head"),
            P(None, "head"),
            P(None, "head"),
            P("head", None),
        ),
        out_specs=P(("ctx", "head"), None),
        check_vma=False,
    )
```

```python
import jax
import jax.numpy as jnp
from jax import lax
from jax.experimental import pallas as pl
from jax.experimental.pallas import tpu as pltpu
from jax.sharding import PartitionSpec as P

HSZ = 128
BAND = 512
STRIDE = 512
HIGHEST = lax.Precision.HIGHEST


def passed_along(block, axis, distance):
    devices = range(lax.axis_size(axis))
    route = [(i - distance, i) for i in devices if i - distance in devices]
    return lax.ppermute(block, axis, route)


def band_kernel(valid_ref, q_ref, k_ref, v_ref, old_k_ref, old_v_ref, out_ref):
    valid = valid_ref[0, 0] > 0
    step = BAND // 2
    across_last = (((1,), (1,)), ((), ()))
    for low in range(0, BAND, step):
        q_rows = q_ref[low : low + step, :]
        old = lax.dot_general(q_rows, old_k_ref[low:, :], across_last, precision=HIGHEST)
        new = lax.dot_general(q_rows, k_ref[: low + step, :], across_last, precision=HIGHEST)
        old_row = lax.broadcasted_iota(jnp.int32, old.shape, 0)
        old_column = lax.broadcasted_iota(jnp.int32, old.shape, 1)
        new_row = lax.broadcasted_iota(jnp.int32, new.shape, 0)
        new_column = lax.broadcasted_iota(jnp.int32, new.shape, 1)
        old = jnp.where((old_column > old_row) & valid, old * HSZ ** (-0.5), -jnp.inf)
        new = jnp.where(new_column <= new_row + low, new * HSZ ** (-0.5), -jnp.inf)
        top = jnp.maximum(
            jnp.max(old, axis=1, keepdims=True), jnp.max(new, axis=1, keepdims=True)
        )
        old, new = jnp.exp(old - top), jnp.exp(new - top)
        total = jnp.sum(old, axis=1, keepdims=True) + jnp.sum(new, axis=1, keepdims=True)
        summed = jnp.dot(
            old, old_v_ref[low:, :], precision=HIGHEST, preferred_element_type=jnp.float32
        ) + jnp.dot(
            new, v_ref[: low + step, :], precision=HIGHEST, preferred_element_type=jnp.float32
        )
        out_ref[low : low + step, :] = summed / total


def band(valid, queries, keys, values, old_k, old_v, first_block, blocks, first_head, heads):
    def own(head, block):
        return first_block + block, first_head + head

    def before(head, block):
        return block, first_head + head

    tile = (BAND, HSZ)
    work = heads * blocks * BAND * BAND * HSZ
    return pl.pallas_call(
        band_kernel,
        grid=(heads, blocks),
        out_shape=jax.ShapeDtypeStruct((blocks * BAND, heads * HSZ), jnp.float32),
        in_specs=[
            pl.BlockSpec(memory_space=pltpu.SMEM),
            pl.BlockSpec(tile, own),
            pl.BlockSpec(tile, own),
            pl.BlockSpec(tile, own),
            pl.BlockSpec(tile, before),
            pl.BlockSpec(tile, before),
        ],
        out_specs=pl.BlockSpec(tile, lambda head, block: (block, head)),
        compiler_params=pltpu.CompilerParams(vmem_limit_bytes=32 * 2**20),
        cost_estimate=pl.CostEstimate(
            flops=36 * work, bytes_accessed=24 * heads * blocks * BAND * HSZ, transcendentals=0
        ),
    )(valid, queries, keys, values, old_k, old_v)


def strided_one(q_two, k_two, v_two):
    scores = jnp.einsum("brd,crd->rbc", q_two, k_two, precision=HIGHEST) * HSZ ** (-0.5)
    count = q_two.shape[0]
    allowed = (
        jnp.arange(count, dtype=jnp.int32)[None, :] <= jnp.arange(count, dtype=jnp.int32)[:, None]
    )
    scores = jnp.where(allowed[None], scores, -jnp.inf)
    top = jnp.max(scores, axis=-1, keepdims=True)
    weights = jnp.exp(scores - top)
    total = jnp.sum(weights, axis=-1)
    summed = jnp.einsum("rbc,crd->brd", weights, v_two, precision=HIGHEST)
    return summed / jnp.transpose(total)[:, :, None]


def matmul(left, right):
    return jnp.dot(left, right, precision=HIGHEST, preferred_element_type=jnp.float32)


def local(queries, keys, values, stride_query_w, stride_key_w, stride_value_w, out_weight):
    rows, width = queries.shape
    heads_here = width // HSZ
    along, across = lax.axis_size("ctx"), lax.axis_size("head")
    own_rows = rows // across
    piece = own_rows // along
    count = rows // BAND
    every = jnp.ones((1, 1), jnp.int32)
    not_first = (lax.axis_index("ctx") > 0).astype(jnp.int32).reshape(1, 1)
    old_k = passed_along(keys[rows - BAND :], "ctx", 1)
    old_v = passed_along(values[rows - BAND :], "ctx", 1)
    groups = 2 if heads_here % 2 == 0 else 1
    part = width // groups
    few = heads_here // groups
    laters = [
        band(every, queries, keys, values, keys, values, 1, count - 1, group * few, few)
        for group in range(groups)
    ]
    maps = (stride_query_w, stride_key_w, stride_value_w)
    sums = [0.0, 0.0, 0.0]
    for group in range(groups):
        start = band(not_first, queries, keys, values, old_k, old_v, 0, 1, group * few, few)
        banded = jnp.concatenate([start, laters[group]], axis=0)
        banded = jnp.transpose(banded.reshape(across, along, piece, part), (1, 0, 2, 3))
        banded = lax.all_to_all(banded, "ctx", split_axis=0, concat_axis=0, tiled=True)
        banded = lax.all_gather(banded.reshape(rows, part), "head", axis=1, tiled=True)
        for at, weight in enumerate(maps):
            met = weight.reshape(across, groups, part, width)[:, group].reshape(-1, width)
            sums[at] = sums[at] + matmul(banded, met)
    grouped = (along * (rows // STRIDE), STRIDE // along, heads_here, HSZ)
    q_two, k_two, v_two = (total.reshape(grouped) for total in sums)
    attended = jax.vmap(strided_one, in_axes=2, out_axes=2)(q_two, k_two, v_two)
    attended = attended.reshape(along, across, piece, width)
    attended = jnp.transpose(attended, (1, 0, 2, 3)).reshape(rows, width)
    columns = out_weight.shape[1] // 4
    quarters = []
    for at in range(0, 4 * columns, columns):
        share = matmul(attended, out_weight[:, at : at + columns])
        mixed = lax.psum_scatter(share, "head", scatter_dimension=0, tiled=True)
        mixed = mixed.reshape(along, piece, columns)
        mixed = lax.all_to_all(mixed, "ctx", split_axis=0, concat_axis=0, tiled=True)
        quarters.append(mixed.reshape(own_rows, columns))
    return jnp.concatenate(quarters, axis=1)


def solution(mesh):
    return jax.shard_map(
        local,
        mesh=mesh,
        in_specs=(
            P("ctx", "head"),
            P("ctx", "head"),
            P("ctx", "head"),
            P(None, "head"),
            P(None, "head"),
            P(None, "head"),
            P("head", None),
        ),
        out_specs=P(("ctx", "head"), None),
        check_vma=False,
    )
```

```python
import jax
import jax.numpy as jnp
from jax import lax
from jax.experimental import pallas as pl
from jax.experimental.pallas import tpu as pltpu
from jax.sharding import PartitionSpec as P

HSZ = 128
BAND = 512
STRIDE = 512
HIGHEST = lax.Precision.HIGHEST


def passed_along(block, axis, distance):
    devices = range(lax.axis_size(axis))
    route = [(i - distance, i) for i in devices if i - distance in devices]
    return lax.ppermute(block, axis, route)


def band_kernel(valid_ref, q_ref, k_ref, v_ref, old_k_ref, old_v_ref, out_ref):
    valid = valid_ref[0, 0] > 0
    step = BAND // 2
    across_last = (((1,), (1,)), ((), ()))
    for low in range(0, BAND, step):
        q_rows = q_ref[low : low + step, :]
        old = lax.dot_general(q_rows, old_k_ref[low:, :], across_last, precision=HIGHEST)
        new = lax.dot_general(q_rows, k_ref[: low + step, :], across_last, precision=HIGHEST)
        old_row = lax.broadcasted_iota(jnp.int32, old.shape, 0)
        old_column = lax.broadcasted_iota(jnp.int32, old.shape, 1)
        new_row = lax.broadcasted_iota(jnp.int32, new.shape, 0)
        new_column = lax.broadcasted_iota(jnp.int32, new.shape, 1)
        old = jnp.where((old_column > old_row) & valid, old * HSZ ** (-0.5), -jnp.inf)
        new = jnp.where(new_column <= new_row + low, new * HSZ ** (-0.5), -jnp.inf)
        top = jnp.maximum(
            jnp.max(old, axis=1, keepdims=True), jnp.max(new, axis=1, keepdims=True)
        )
        old, new = jnp.exp(old - top), jnp.exp(new - top)
        total = jnp.sum(old, axis=1, keepdims=True) + jnp.sum(new, axis=1, keepdims=True)
        summed = jnp.dot(
            old, old_v_ref[low:, :], precision=HIGHEST, preferred_element_type=jnp.float32
        ) + jnp.dot(
            new, v_ref[: low + step, :], precision=HIGHEST, preferred_element_type=jnp.float32
        )
        out_ref[low : low + step, :] = summed / total


def band(valid, queries, keys, values, old_k, old_v, first_block, blocks, first_head, heads):
    def own(head, block):
        return first_block + block, first_head + head

    def before(head, block):
        return block, first_head + head

    tile = (BAND, HSZ)
    work = heads * blocks * BAND * BAND * HSZ
    return pl.pallas_call(
        band_kernel,
        grid=(heads, blocks),
        out_shape=jax.ShapeDtypeStruct((blocks * BAND, heads * HSZ), jnp.float32),
        in_specs=[
            pl.BlockSpec(memory_space=pltpu.SMEM),
            pl.BlockSpec(tile, own),
            pl.BlockSpec(tile, own),
            pl.BlockSpec(tile, own),
            pl.BlockSpec(tile, before),
            pl.BlockSpec(tile, before),
        ],
        out_specs=pl.BlockSpec(tile, lambda head, block: (block, head)),
        compiler_params=pltpu.CompilerParams(vmem_limit_bytes=32 * 2**20),
        cost_estimate=pl.CostEstimate(
            flops=36 * work, bytes_accessed=24 * heads * blocks * BAND * HSZ, transcendentals=0
        ),
    )(valid, queries, keys, values, old_k, old_v)


def strided_one(q_two, k_two, v_two):
    scores = jnp.einsum("brd,crd->rbc", q_two, k_two, precision=HIGHEST) * HSZ ** (-0.5)
    count = q_two.shape[0]
    allowed = (
        jnp.arange(count, dtype=jnp.int32)[None, :] <= jnp.arange(count, dtype=jnp.int32)[:, None]
    )
    scores = jnp.where(allowed[None], scores, -jnp.inf)
    top = jnp.max(scores, axis=-1, keepdims=True)
    weights = jnp.exp(scores - top)
    total = jnp.sum(weights, axis=-1)
    summed = jnp.einsum("rbc,crd->brd", weights, v_two, precision=HIGHEST)
    return summed / jnp.transpose(total)[:, :, None]


def matmul(left, right, precision=HIGHEST):
    return jnp.dot(left, right, precision=precision, preferred_element_type=jnp.float32)


def local(queries, keys, values, stride_query_w, stride_key_w, stride_value_w, out_weight):
    rows, width = queries.shape
    heads_here = width // HSZ
    along, across = lax.axis_size("ctx"), lax.axis_size("head")
    own_rows = rows // across
    piece = own_rows // along
    count = rows // BAND
    every = jnp.ones((1, 1), jnp.int32)
    not_first = (lax.axis_index("ctx") > 0).astype(jnp.int32).reshape(1, 1)
    old_k = passed_along(keys[rows - BAND :], "ctx", 1)
    old_v = passed_along(values[rows - BAND :], "ctx", 1)
    groups = 4 if heads_here % 4 == 0 else 2 if heads_here % 2 == 0 else 1
    part = width // groups
    few = heads_here // groups
    laters = [
        band(every, queries, keys, values, keys, values, 1, count - 1, group * few, few)
        for group in range(groups)
    ]
    maps = (stride_query_w, stride_key_w, stride_value_w)
    sums = [0.0, 0.0, 0.0]
    for group in range(groups):
        start = band(not_first, queries, keys, values, old_k, old_v, 0, 1, group * few, few)
        banded = jnp.concatenate([start, laters[group]], axis=0)
        banded = jnp.transpose(banded.reshape(across, along, piece, part), (1, 0, 2, 3))
        banded = lax.all_to_all(banded, "ctx", split_axis=0, concat_axis=0, tiled=True)
        banded = lax.all_gather(banded.reshape(rows, part), "head", axis=1, tiled=True)
        for at, weight in enumerate(maps):
            met = weight.reshape(across, groups, part, width)[:, group].reshape(-1, width)
            how = lax.Precision.HIGH if at == 2 else HIGHEST
            sums[at] = sums[at] + matmul(banded, met, how)
    grouped = (along * (rows // STRIDE), STRIDE // along, heads_here, HSZ)
    q_two, k_two, v_two = (total.reshape(grouped) for total in sums)
    attended = jax.vmap(strided_one, in_axes=2, out_axes=2)(q_two, k_two, v_two)
    attended = attended.reshape(along, across, piece, width)
    attended = jnp.transpose(attended, (1, 0, 2, 3)).reshape(rows, width)
    columns = out_weight.shape[1] // 4
    quarters = []
    for at in range(0, 4 * columns, columns):
        share = matmul(attended, out_weight[:, at : at + columns])
        mixed = lax.psum_scatter(share, "head", scatter_dimension=0, tiled=True)
        mixed = mixed.reshape(along, piece, columns)
        mixed = lax.all_to_all(mixed, "ctx", split_axis=0, concat_axis=0, tiled=True)
        quarters.append(mixed.reshape(own_rows, columns))
    return jnp.concatenate(quarters, axis=1)


def solution(mesh):
    return jax.shard_map(
        local,
        mesh=mesh,
        in_specs=(
            P("ctx", "head"),
            P("ctx", "head"),
            P("ctx", "head"),
            P(None, "head"),
            P(None, "head"),
            P(None, "head"),
            P("head", None),
        ),
        out_specs=P(("ctx", "head"), None),
        check_vma=False,
    )
```
